256 devices in a mesh: branch: 8 (over y, core), slot: 32 (over x, z).
Axes of the slice: x: 4, y: 4, z: 8, core: 2. Of those that a mesh axis runs over, the one named last changes fastest.
Arguments:
- kkt_inverse: bfloat16 [2048, 2048], replicated
- cost: float32 [16384, 2048], P(('branch', 'slot'))
- anchor: float32 [16384, 2048], P(('branch', 'slot')), may hold values from 0 to 2
- capacity: float32 [16384, 2048], P(('branch', 'slot')), may hold values from 0.5 to 3
- multiplier: float32 [16384, 1536], P(('branch', 'slot')), may hold values from -3 to 3
- penalty: float32 [2048], replicated, may hold values from 0.5 to 2
- weight: int32 [16384], P(('branch', 'slot')), may hold values from 1 to 16
- node_two: int32 [16384], P(('branch', 'slot')), may hold values from 0 to 255, as said below
- node_three: int32 [16384], P(('branch', 'slot')), may hold values from 0 to 1023, as said below
Outputs:
- solution: float32 [16384, 2048], P(('branch', 'slot'))
- new_multiplier: float32 [16384, 1536], P(('branch', 'slot'))
The draws below stay inside these ranges and needn't reach their ends.
Inputs may be any that keep to these rules, and one draw needn't show every extreme that they name: `node_three`: scenarios g * 2048 to (g + 1) * 2048 - 1 have section-three ids g * 128 to (g + 1) * 128 - 1, never falling along the scenarios, every id used. `node_two`: scenarios g * 2048 to (g + 1) * 2048 - 1 have section-two ids g * 32 to (g + 1) * 32 - 1, never falling along the scenarios, every id used; all scenarios of one section-three node share one section-two node.
All inputs are finite; a program needn't handle non-finite values.
Results may differ from the reference program's by a relative error of at most 0.0031.
Values sent between devices are 32-bit elements; how exact they have to be, the bound alone decides.
A program may use at most 64 MiB of HBM per device.

```python
import math
import jax
import jax.numpy as jnp
from jax import lax

NV = 2048
SECTION_VARS = 512
NODE3_GRP = 128
NODE2_GRP = 32
ITERS = 8
GROUP = 2048
SCENARIOS = 16384
NODE3 = 1024
NODE2 = 256


def tree_orders(key):
    group_count = SCENARIOS // GROUP
    group_keys = jax.random.split(key, group_count)
    return jax.vmap(lambda single: jax.random.permutation(single, GROUP - 1))(group_keys)


def tree_labels(orders, per_group):
    group_count = orders.shape[0]
    marks = (orders < per_group - 1).astype(jnp.int32)
    marks = jnp.concatenate([jnp.zeros((group_count, 1), jnp.int32), marks], axis=1)
    labels = jnp.cumsum(marks, axis=1) + jnp.arange(group_count, dtype=jnp.int32)[:, None] * per_group
    return labels.reshape(-1).astype(jnp.int32)


def draw_node_two(key, part):
    return tree_labels(tree_orders(key), NODE2_GRP)


def draw_node_three(key, part):
    return tree_labels(tree_orders(key), NODE3_GRP)


def draw_kkt_inverse(key, part):
    key = jax.random.fold_in(key, 11)
    diag_key, off_key = jax.random.split(key)
    diagonal = jnp.exp(jax.random.uniform(diag_key, (NV,), jnp.float32, jnp.log(0.4), jnp.log(0.95)))
    offdiag = jax.random.normal(off_key, (NV, NV), jnp.float32) * (0.2 / NV ** 0.5)
    matrix = offdiag + jnp.eye(NV, dtype=jnp.float32) * diagonal[None, :]
    return matrix.astype(jnp.bfloat16)


def draw_cost(key, part):
    key = jax.random.fold_in(key, 12)
    branch_key, noise_key = jax.random.split(key)
    group_count = SCENARIOS // GROUP
    offsets = jax.random.normal(branch_key, (group_count, NV), jnp.float32)
    noise = jax.random.normal(noise_key, (SCENARIOS, NV), jnp.float32) * 0.7
    return jnp.repeat(offsets, GROUP, axis=0) + noise


def with_ends(entries, rng, smallest, high):
    index_at = [jax.random.randint(jax.random.fold_in(rng, axis), (), 0, length) for axis, length in enumerate(entries.shape)]
    main_axis = entries.shape.index(max(entries.shape))
    neighbour = index_at[:main_axis] + [(index_at[main_axis] + 1) % entries.shape[main_axis]] + index_at[main_axis + 1:]
    return entries.at[tuple(index_at)].set(smallest).at[tuple(neighbour)].set(high)


def block_scale(own_key, dims, cuts, smallest, high):
    def one(dim, parts):
        heights = jax.random.uniform(jax.random.fold_in(jax.random.fold_in(own_key, 6), dim), (parts,), jnp.float32, smallest / len(cuts), high / len(cuts))
        return jnp.repeat(jnp.exp(heights), dims[dim] // parts).reshape((-1,) + (1,) * (len(dims) - dim - 1))

    gain = one(*cuts[0])
    for cut in cuts[1:]:
        gain = gain * one(*cut)
    return gain


def gaussian(stream_key, dims, spread, bound, cuts=(), kind=jnp.bfloat16):
    gain = block_scale(stream_key, dims, cuts, -0.22, 0.18) if cuts else 1.0
    result = jax.random.normal(stream_key, dims, jnp.float32) * spread * gain
    return jnp.minimum(jnp.maximum(result, -bound), bound).astype(kind)


def setup_inputs(seed: int = 0) -> dict:
    seeds = jax.random.split(jax.random.key(seed), 10)
    return {
        "kkt_inverse": draw_kkt_inverse(jax.random.fold_in(seeds[9], 71), 0),
        "cost": draw_cost(jax.random.fold_in(seeds[9], 71), 0),
        "anchor": jnp.clip(2.0 * jax.random.uniform(seeds[2], (SCENARIOS, NV), jnp.float32) ** block_scale(seeds[2], (SCENARIOS, NV), ((0, 256),), -0.2, 0.2), 0.0, 2.0),
        "capacity": jnp.clip(0.5 + 2.5 * jax.random.uniform(seeds[3], (SCENARIOS, NV), jnp.float32) ** block_scale(seeds[3], (SCENARIOS, NV), ((0, 256),), -0.2, 0.2), 0.5, 3.0),
        "multiplier": gaussian(seeds[4], (SCENARIOS, 3 * SECTION_VARS), 0.5, 3.0, ((0, 256),), jnp.float32),
        "penalty": jnp.clip(jnp.exp(jax.random.uniform(seeds[5], (NV,), jnp.float32, math.log(0.5), math.log(2.0))), 0.5, 2.0),
        "weight": with_ends(jax.random.randint(seeds[6], (SCENARIOS,), 1, 17), jax.random.fold_in(seeds[6], 1), 1, 16).astype(jnp.int32),
        "node_two": draw_node_two(jax.random.fold_in(seeds[9], 71), 0),
        "node_three": draw_node_three(jax.random.fold_in(seeds[9], 71), 0),
    }


admm_sigma = 1.0


def section_means(values, chances, labels, count):
    sums = jax.ops.segment_sum(chances[:, None] * values, labels, num_segments=count)
    totals = jax.ops.segment_sum(chances, labels, num_segments=count)
    means = sums / totals[:, None]
    return means[labels]


def reference(kkt_inverse, cost, anchor, capacity, multiplier, penalty, weight, node_two, node_three):
    scen_count = cost.shape[0]
    padded = jnp.concatenate([multiplier, jnp.zeros((scen_count, SECTION_VARS), jnp.float32)], axis=1)
    linear = cost + padded - penalty[None, :] * anchor
    inverse_wide = kkt_inverse.astype(jnp.float32)
    box = jnp.clip(anchor, 0.0, capacity)
    scaled = jnp.zeros_like(box)
    for iteration in range(ITERS):
        rhs_value = (admm_sigma * (box - scaled) - linear).astype(jnp.bfloat16).astype(jnp.float32)
        trial = jnp.dot(rhs_value, inverse_wide, precision=lax.Precision.HIGHEST)
        box = jnp.clip(trial + scaled, 0.0, capacity)
        scaled = scaled + trial - box
    chances = weight.astype(jnp.float32)
    root_mean = jnp.sum(chances[:, None] * box[:, :SECTION_VARS], axis=0) / jnp.sum(chances)
    root_rows = jnp.broadcast_to(root_mean[None, :], (scen_count, SECTION_VARS))
    second = section_means(box[:, SECTION_VARS:2 * SECTION_VARS], chances, node_two, NODE2)
    third = section_means(box[:, 2 * SECTION_VARS:3 * SECTION_VARS], chances, node_three, NODE3)
    consensus = jnp.concatenate([root_rows, second, third], axis=1)
    new_multiplier = multiplier + penalty[None, :3 * SECTION_VARS] * (box[:, :3 * SECTION_VARS] - consensus)
    return box, new_multiplier
```

```python
import functools

import jax
import jax.numpy as jnp
from jax import lax
from jax.experimental import pallas as pl
from jax.experimental.pallas import tpu as pltpu
from jax.sharding import PartitionSpec as P

ITERS = 8
ROWS = 64
NV = 2048
SEC = 512
BLK = 256
NBLK = NV // BLK
NX, NY, NZ, NC = 4, 4, 8, 2
F32 = jnp.float32
BF16 = jnp.bfloat16
ORDER = (2, 3, 4, 5, 0, 1, 6, 7)


def split2(v):
    hi = v.astype(BF16)
    lo = (v - hi.astype(F32)).astype(BF16)
    return hi, lo


def stack3(v):
    hi, lo = split2(v)
    rest = (v - hi.astype(F32) - lo.astype(F32)).astype(BF16)
    return jnp.concatenate([hi, lo, rest], axis=0)


def mm(a, b):
    return jnp.dot(a, b, preferred_element_type=F32)


def triple(a):
    a = a.astype(BF16)
    return jnp.concatenate([a, a, a], axis=1)


def wait_bytes(ref, sem):
    pltpu.make_async_copy(ref, ref, sem).wait()


def kernel(
    k_h, cost_h, anchor_h, cap_h, mult_h, pen_h, w_h, n2_h, n3_h,
    sol_h, nm_h,
    kv, cost, anchor, cap, mult, pen, wv, n2v, n3v,
    lin, sc, box, rhs, nm,
    coef_a, coef_l, coef_w, coef_c, coef_d, inv,
    meta1, meta1_in, meta2, meta2_in,
    pay1, pay1_in, pay2, pay2_in,
    root1, root1_in, root2, root2_in,
    in_sem, k_sem, out_sem, send_sem, recv_sem,
):
    slot = lax.axis_index("slot")
    branch = lax.axis_index("branch")
    x, z = slot // NZ, slot % NZ
    y, core = branch // NC, branch % NC

    z_peers = [{"slot": x * NZ + (z + d) % NZ} for d in range(1, NZ)]
    x_peers = [{"slot": ((x + d) % NX) * NZ + z} for d in range(1, NX)]
    zc_peers = [
        {"slot": x * NZ + (z + d) % NZ, "branch": y * NC + (core + e) % NC}
        for d in range(NZ) for e in range(NC) if d or e
    ]
    xy_peers = [
        {"slot": ((x + d) % NX) * NZ + z, "branch": ((y + e) % NY) * NC + core}
        for d in range(NX) for e in range(NY) if d or e
    ]

    ins = [
        pltpu.make_async_copy(a, b, in_sem.at[i])
        for i, (a, b) in enumerate((
            (cost_h, cost), (anchor_h, anchor), (mult_h, mult), (pen_h, pen), (cap_h, cap),
            (w_h, wv), (n2_h, n2v), (n3_h, n3v),
        ))
    ]
    for c in ins:
        c.start()
    ks = [
        pltpu.make_async_copy(
            k_h.at[:, pl.ds(j * BLK, BLK)], kv.at[:, pl.ds(j * BLK, BLK)], k_sem.at[j]
        )
        for j in range(NBLK)
    ]
    for c in ks:
        c.start()

    barrier = pltpu.get_barrier_semaphore()
    for peer in zc_peers + xy_peers:
        pl.semaphore_signal(barrier, inc=1, device_id=peer, device_id_type=pl.DeviceIdType.MESH)

    def gather_start(src, dst, peers, index):
        for peer in peers:
            pltpu.make_async_remote_copy(
                src_ref=src, dst_ref=dst, send_sem=send_sem.at[index], recv_sem=recv_sem.at[index],
                device_id=peer, device_id_type=pl.DeviceIdType.MESH,
            ).start()

    for c in ins:
        c.wait()

    start = jnp.clip(anchor[...], 0.0, cap[...])
    lin[:, : 3 * SEC] = (
        cost[:, : 3 * SEC] + mult[...] - pen[:, : 3 * SEC] * anchor[:, : 3 * SEC]
    )
    lin[:, 3 * SEC :] = cost[:, 3 * SEC :] - pen[:, 3 * SEC :] * anchor[:, 3 * SEC :]
    sc[...] = jnp.zeros((ROWS, NV), F32)
    rhs[0] = (start - lin[...]).astype(BF16)

    def block(j, cur, nxt, last):
        s = slice(j * BLK, (j + 1) * BLK)
        trial = jnp.dot(rhs[cur], kv[:, s], preferred_element_type=F32)
        total = trial + sc[:, s]
        new = jnp.clip(total, 0.0, cap[:, s])
        if last:
            box[:, s] = new
            return new
        rest = total - new
        sc[:, s] = rest
        rhs[nxt, :, s] = ((new - rest) - lin[:, s]).astype(BF16)
        return new

    def step(i):
        for j in range(NBLK):
            if i == 0:
                ks[j].wait()
            block(j, i % 2, 1 - i % 2, False)

    step(0)

    w_row = wv[...].astype(F32)
    ids = (n2v[...].astype(F32), n3v[...].astype(F32))
    eye = lax.broadcasted_iota(jnp.int32, (ROWS, ROWS), 0) == lax.broadcasted_iota(
        jnp.int32, (ROWS, ROWS), 1
    )
    sub = lax.broadcasted_iota(jnp.int32, (8, ROWS), 0)
    lane = lax.broadcasted_iota(jnp.int32, (8, 128), 1)
    row8 = lax.broadcasted_iota(jnp.int32, (8, 128), 0)
    id_cols, local_totals, ends = [], [], []
    for t in range(2):
        id_col = jnp.sum(jnp.where(eye, ids[t], 0.0), axis=1, keepdims=True)
        id_cols.append(id_col)
        same = jnp.where(id_col == ids[t], w_row, 0.0)
        coef_l[t] = triple(same)
        local_totals.append(jnp.sum(same, axis=1, keepdims=True))
        first, final = ids[t][:, 0:1], ids[t][:, ROWS - 1 : ROWS]
        at_first = jnp.where(ids[t] == first, w_row, 0.0)
        at_final = jnp.where((ids[t] == final) & (final != first), w_row, 0.0)
        ends.append((first, final, jnp.sum(at_first, axis=1, keepdims=True),
                     jnp.sum(at_final, axis=1, keepdims=True)))
        for h in range(2):
            q = 4 * h + 2 * t
            rows = jnp.where(sub == q, at_first, jnp.where(sub == q + 1, at_final, 0.0))
            coef_a[2 * t + h] = triple(rows)
    for h in range(2):
        coef_w[h] = triple(jnp.where((sub == 2 * h) | (sub == 2 * h + 1), w_row, 0.0))
    weight_sum = jnp.sum(w_row, axis=1, keepdims=True)

    q_lane = lane % 4
    own_ids = jnp.where(
        q_lane == 0, ends[0][0], jnp.where(q_lane == 1, ends[0][1],
        jnp.where(q_lane == 2, ends[1][0], ends[1][1])))
    own_weights = jnp.where(
        q_lane == 0, ends[0][2], jnp.where(q_lane == 1, ends[0][3],
        jnp.where(q_lane == 2, ends[1][2], ends[1][3])))
    message = jnp.where(row8 == 0, own_ids, jnp.where(row8 == 1, own_weights, 0.0))
    message = jnp.where((lane < 64) & (lane // 8 == z), message, 0.0)
    meta1[...] = message
    meta1_in[z] = message

    pl.semaphore_wait(barrier, len(zc_peers) + len(xy_peers))
    gather_start(meta1, meta1_in.at[z], z_peers, 0)
    step(1)
    step(2)

    wait_bytes(meta1_in.at[pl.ds(0, NZ - 1)], recv_sem.at[0])
    line = jnp.sum(meta1_in[...], axis=0)
    line_ids, line_w = line[0:1], line[1:2]
    odd = row8 % 2 == 1
    targ = jnp.sum(
        jnp.where(lane == row8 + jnp.where(odd, 56, 0), line_ids, 0.0), axis=1, keepdims=True
    )
    before = jnp.sum(jnp.where(lane == row8 - 1, line_ids, 0.0), axis=1, keepdims=True)
    group = (lane < 64) & ((lane % 8) // 2 == row8 // 2)
    keep = jnp.logical_not(odd) | (targ != before)
    spread = jnp.where(group & keep & (line_ids == targ), 1.0, 0.0)
    line_weight = jnp.sum(spread * line_w, axis=1, keepdims=True)
    place = lane == 64 + x * 8 + row8
    put_ids = jnp.sum(jnp.where(place, targ, 0.0), axis=0, keepdims=True)
    put_w = jnp.sum(jnp.where(place, line_weight, 0.0), axis=0, keepdims=True)
    message = jnp.where(row8 == 0, put_ids, jnp.where(row8 == 1, put_w, 0.0))
    meta2[...] = message
    meta2_in[x] = message
    coef_d[...] = (spread + pltpu.roll(spread, 64, 1)).astype(BF16)
    gather_start(meta2, meta2_in.at[x], x_peers, 1)
    step(3)
    step(4)

    wait_bytes(meta2_in.at[pl.ds(0, NX - 1)], recv_sem.at[1])
    table = line + jnp.sum(meta2_in[...], axis=0)
    all_ids, all_w = table[0:1], table[1:2]
    wide = lax.broadcasted_iota(jnp.int32, (ROWS, 128), 1)
    other = ((wide < 64) & (wide // 8 != z)) | (
        (wide >= 64) & (wide < 96) & ((wide - 64) // 8 != x)
    )
    for t in range(2):
        match = (id_cols[t] == all_ids) & other & ((wide % 4) // 2 == t)
        for h in range(2):
            part = jnp.where(match & ((wide % 8) // 4 == h), 1.0, 0.0)
            if h == 0:
                total = local_totals[t] + jnp.sum(part * all_w, axis=1, keepdims=True)
                inv[:, 128 * t : 128 * t + 128] = jnp.broadcast_to(1.0 / total, (ROWS, 128))
            half = part.astype(BF16)
            q = 2 * t + h
            coef_c[q * ROWS : (q + 1) * ROWS] = jnp.concatenate([half, half], axis=1)
    step(5)
    step(6)

    outs = []
    nodes = jnp.zeros((8, BLK), F32)
    roots = jnp.where(row8 == 4, weight_sum, 0.0)
    for n, j in enumerate(ORDER):
        new = block(j, 1, 0, True)
        s = pl.ds(j * BLK, BLK)
        out = pltpu.make_async_copy(box.at[:, s], sol_h.at[:, s], out_sem.at[j])
        out.start()
        outs.append(out)
        if j < 2:
            part = mm(coef_w[j], stack3(new))
            roots = jnp.where(row8 == 2 * j, part[:, :128], roots)
            roots = jnp.where(row8 == 2 * j + 1, part[:, 128:], roots)
            if j == 1:
                root1[...] = roots
                root1_in[z * NC + core] = roots
                gather_start(root1, root1_in.at[z * NC + core], zc_peers, 4)
        elif j < 6:
            nodes = nodes + mm(coef_a[j - 2], stack3(new))
            if j == 5:
                pay1[...] = nodes
                pay1_in[z] = nodes
                gather_start(pay1, pay1_in.at[z], z_peers, 2)

    for t in range(2):
        for h in range(2):
            c = SEC * (t + 1) + BLK * h
            s = slice(c, c + BLK)
            local = mm(coef_l[t], stack3(box[:, s]))
            scale = inv[:, 128 * t : 128 * t + 1]
            nm[:, s] = mult[:, s] + pen[:, s] * (box[:, s] - local * scale)
    nm[:, :SEC] = mult[:, :SEC] + pen[:, :SEC] * box[:, :SEC]

    wait_bytes(pay1_in.at[pl.ds(0, NZ - 1)], recv_sem.at[2])
    hi1, lo1 = split2(pay1_in[...].reshape(NZ * 8, BLK))
    nodes = mm(coef_d[...], jnp.concatenate([hi1, lo1], axis=0))
    pay2[...] = nodes
    pay2_in[x] = nodes
    gather_start(pay2, pay2_in.at[x], x_peers, 3)

    wait_bytes(root1_in.at[pl.ds(0, NZ * NC - 1)], recv_sem.at[4])
    roots = jnp.sum(root1_in[...], axis=0)
    root2[...] = roots
    root2_in[x * NY + y] = roots
    gather_start(root2, root2_in.at[x * NY + y], xy_peers, 5)

    wait_bytes(pay2_in.at[pl.ds(0, NX - 1)], recv_sem.at[3])
    hi2, lo2 = split2(pay2_in[...].reshape(NX * 8, BLK))
    none = jnp.zeros((32, BLK), BF16)
    stacked = jnp.concatenate([hi1, hi2, none, lo1, lo2, none], axis=0)
    remote = mm(coef_c[...], stacked)
    for t in range(2):
        for h in range(2):
            c = SEC * (t + 1) + BLK * h
            s = slice(c, c + BLK)
            q = 2 * t + h
            scale = inv[:, 128 * t : 128 * t + 1]
            nm[:, s] = nm[:, s] - pen[:, s] * (remote[q * ROWS : (q + 1) * ROWS] * scale)
    out = pltpu.make_async_copy(
        nm.at[:, pl.ds(SEC, 2 * SEC)], nm_h.at[:, pl.ds(SEC, 2 * SEC)], out_sem.at[NBLK]
    )
    out.start()
    outs.append(out)

    wait_bytes(root2_in.at[pl.ds(0, NX * NY - 1)], recv_sem.at[5])
    roots = jnp.sum(root2_in[...], axis=0)
    means = roots / roots[4:5]
    for r in range(4):
        s = slice(128 * r, 128 * r + 128)
        nm[:, s] = nm[:, s] - pen[:, s] * means[r : r + 1]
    out = pltpu.make_async_copy(
        nm.at[:, pl.ds(0, SEC)], nm_h.at[:, pl.ds(0, SEC)], out_sem.at[NBLK + 1]
    )
    out.start()
    outs.append(out)

    for index, ref in enumerate((
        meta1_in.at[pl.ds(0, NZ - 1)], meta2_in.at[pl.ds(0, NX - 1)],
        pay1_in.at[pl.ds(0, NZ - 1)], pay2_in.at[pl.ds(0, NX - 1)],
        root1_in.at[pl.ds(0, NZ * NC - 1)], root2_in.at[pl.ds(0, NX * NY - 1)],
    )):
        wait_bytes(ref, send_sem.at[index])
    for out in outs:
        out.wait()


def on_device(
    kkt_inverse, cost, anchor, capacity, multiplier, penalty, weight, node_two, node_three
):
    anywhere = pl.BlockSpec(memory_space=pl.ANY)
    vm = pltpu.VMEM
    return pl.pallas_call(
        kernel,
        out_shape=(
            jax.ShapeDtypeStruct((ROWS, NV), F32),
            jax.ShapeDtypeStruct((ROWS, 3 * SEC), F32),
        ),
        in_specs=[anywhere] * 9,
        out_specs=(anywhere, anywhere),
        scratch_shapes=[
            vm((NV, NV), BF16), vm((ROWS, NV), F32), vm((ROWS, NV), F32), vm((ROWS, NV), F32),
            vm((ROWS, 3 * SEC), F32), vm((1, NV), F32),
            vm((1, ROWS), jnp.int32), vm((1, ROWS), jnp.int32), vm((1, ROWS), jnp.int32),
            vm((ROWS, NV), F32), vm((ROWS, NV), F32), vm((ROWS, NV), F32),
            vm((2, ROWS, NV), BF16), vm((ROWS, 3 * SEC), F32),
            vm((4, 8, 192), BF16), vm((2, ROWS, 192), BF16), vm((2, 8, 192), BF16),
            vm((4 * ROWS, 256), BF16), vm((8, 128), BF16), vm((ROWS, 256), F32),
            vm((8, 128), F32), vm((NZ, 8, 128), F32), vm((8, 128), F32), vm((NX, 8, 128), F32),
            vm((8, BLK), F32), vm((NZ, 8, BLK), F32), vm((8, BLK), F32), vm((NX, 8, BLK), F32),
            vm((8, 128), F32), vm((NZ * NC, 8, 128), F32),
            vm((8, 128), F32), vm((NX * NY, 8, 128), F32),
            pltpu.SemaphoreType.DMA((8,)), pltpu.SemaphoreType.DMA((NBLK,)),
            pltpu.SemaphoreType.DMA((NBLK + 2,)),
            pltpu.SemaphoreType.DMA((6,)), pltpu.SemaphoreType.DMA((6,)),
        ],
        compiler_params=pltpu.CompilerParams(
            collective_id=0, has_side_effects=True, vmem_limit_bytes=64 << 20
        ),
        cost_estimate=pl.CostEstimate(
            flops=2 * ITERS * ROWS * NV * NV, bytes_accessed=12 << 20, transcendentals=0
        ),
    )(
        kkt_inverse, cost, anchor, capacity, multiplier, penalty.reshape(1, NV),
        weight.reshape(1, ROWS), node_two.reshape(1, ROWS), node_three.reshape(1, ROWS),
    )


def solution(mesh):
    rows = P(("branch", "slot"), None)
    flat = P(("branch", "slot"))
    return jax.shard_map(
        on_device,
        mesh=mesh,
        in_specs=(P(), rows, rows, rows, rows, P(), flat, flat, flat),
        out_specs=(rows, rows),
        check_vma=False,
    )
```

```python
import functools

import jax
import jax.numpy as jnp
from jax import lax
from jax.experimental import pallas as pl
from jax.experimental.pallas import tpu as pltpu
from jax.sharding import PartitionSpec as P

ITERS = 8
ROWS = 64
NV = 2048
SEC = 512
BLK = 256
NBLK = NV // BLK
NX, NY, NZ, NC = 4, 4, 8, 2
F32 = jnp.float32
BF16 = jnp.bfloat16
XY_FAR_FIRST = (
    (2, 2), (2, 1), (2, 3), (1, 2), (3, 2), (2, 0), (0, 2), (1, 1), (1, 3), (3, 1), (3, 3),
    (1, 0), (3, 0), (0, 1), (0, 3),
)


def split2(v):
    hi = v.astype(BF16)
    lo = (v - hi.astype(F32)).astype(BF16)
    return hi, lo


def stack3(v):
    hi, lo = split2(v)
    rest = (v - hi.astype(F32) - lo.astype(F32)).astype(BF16)
    return jnp.concatenate([hi, lo, rest], axis=0)


def mm(a, b):
    return jnp.dot(a, b, preferred_element_type=F32)


def triple(a):
    a = a.astype(BF16)
    return jnp.concatenate([a, a, a], axis=1)


def wait_bytes(ref, sem):
    pltpu.make_async_copy(ref, ref, sem).wait()


def kernel(
    k_h, cost_h, anchor_h, cap_h, mult_h, pen_h, w_h, n2_h, n3_h,
    box, nm,
    kv, cost, anchor, cap, mult, pen, wv, n2v, n3v,
    lin, sc, rhs,
    coef_l, coef_c, coef_d, mask, inv,
    meta1, meta1_in, meta2, meta2_in,
    pay1, pay1_in, pay2, pay2_in,
    root1, root1_in, root2, root2_in, root3, root3_in,
    in_sem, k_sem, send_sem, recv_sem,
):
    slot = lax.axis_index("slot")
    branch = lax.axis_index("branch")
    x, z = slot // NZ, slot % NZ
    y, core = branch // NC, branch % NC

    z_peers = [{"slot": x * NZ + (z + d) % NZ} for d in (4, 3, 5, 2, 6, 1, 7)]
    x_peers = [{"slot": ((x + d) % NX) * NZ + z} for d in (2, 1, 3)]
    xy_peers = [
        {"slot": ((x + d) % NX) * NZ + z, "branch": ((y + e) % NY) * NC + core}
        for d, e in XY_FAR_FIRST
    ]
    c_peers = [{"branch": y * NC + 1 - core}]
    peers = z_peers + xy_peers + c_peers

    ins = [
        pltpu.make_async_copy(a, b, in_sem.at[i])
        for i, (a, b) in enumerate((
            (cost_h, cost), (anchor_h, anchor), (mult_h, mult), (pen_h, pen), (cap_h, cap),
            (w_h, wv), (n2_h, n2v), (n3_h, n3v),
        ))
    ]
    for c in ins:
        c.start()
    ks = [
        pltpu.make_async_copy(
            k_h.at[:, pl.ds(j * BLK, BLK)], kv.at[:, pl.ds(j * BLK, BLK)], k_sem.at[j]
        )
        for j in range(NBLK)
    ]
    for c in ks:
        c.start()

    barrier = pltpu.get_barrier_semaphore()

    def greet(some):
        for peer in some:
            pl.semaphore_signal(
                barrier, inc=1, device_id=peer, device_id_type=pl.DeviceIdType.MESH
            )

    greet(peers[:8])

    def gather_start(src, dst, peers, index):
        for peer in peers:
            pltpu.make_async_remote_copy(
                src_ref=src, dst_ref=dst, send_sem=send_sem.at[index], recv_sem=recv_sem.at[index],
                device_id=peer, device_id_type=pl.DeviceIdType.MESH,
            ).start()

    for c in ins:
        c.wait()

    start = jnp.clip(anchor[...], 0.0, cap[...])
    lin[:, : 3 * SEC] = (
        cost[:, : 3 * SEC] + mult[...] - pen[:, : 3 * SEC] * anchor[:, : 3 * SEC]
    )
    lin[:, 3 * SEC :] = cost[:, 3 * SEC :] - pen[:, 3 * SEC :] * anchor[:, 3 * SEC :]
    sc[...] = jnp.zeros((ROWS, NV), F32)
    rhs[0] = (start - lin[...]).astype(BF16)

    def block(j, cur, nxt, last):
        s = slice(j * BLK, (j + 1) * BLK)
        trial = jnp.dot(rhs[cur], kv[:, s], preferred_element_type=F32)
        total = trial + sc[:, s]
        new = jnp.clip(total, 0.0, cap[:, s])
        if last:
            box[:, s] = new
            return new
        rest = total - new
        sc[:, s] = rest
        rhs[nxt, :, s] = ((new - rest) - lin[:, s]).astype(BF16)
        return new

    def step(i):
        for j in range(NBLK):
            if i == 0:
                greet(peers[8 + 2 * j : 10 + 2 * j])
                ks[j].wait()
            block(j, i % 2, 1 - i % 2, False)

    step(0)

    w_row = wv[...].astype(F32)
    ids = (n2v[...].astype(F32), n3v[...].astype(F32))
    eye = lax.broadcasted_iota(jnp.int32, (ROWS, ROWS), 0) == lax.broadcasted_iota(
        jnp.int32, (ROWS, ROWS), 1
    )

    def column(row):
        col = jnp.sum(jnp.where(eye, row, 0.0), axis=1, keepdims=True)
        return jnp.broadcast_to(col, (ROWS, 128))

    lane = lax.broadcasted_iota(jnp.int32, (8, 128), 1)
    row8 = lax.broadcasted_iota(jnp.int32, (8, 128), 0)
    id_cols, local_totals, ends = [], [], []
    for t in range(2):
        id_col = jnp.sum(jnp.where(eye, ids[t], 0.0), axis=1, keepdims=True)
        id_cols.append(id_col)
        same = jnp.where(id_col == ids[t], w_row, 0.0)
        coef_l[t] = triple(same)
        local_totals.append(jnp.sum(same, axis=1, keepdims=True))
        first, final = ids[t][:, 0:1], ids[t][:, ROWS - 1 : ROWS]
        at_first = jnp.where(ids[t] == first, w_row, 0.0)
        at_final = jnp.where((ids[t] == final) & (final != first), w_row, 0.0)
        ends.append((first, final, jnp.sum(at_first, axis=1, keepdims=True),
                     jnp.sum(at_final, axis=1, keepdims=True)))
        mask[2 * t] = column(at_first)
        mask[2 * t + 1] = column(at_final)
    mask[4] = column(w_row)
    weight_sum = jnp.sum(w_row, axis=1, keepdims=True)

    q_lane = lane % 4
    own_ids = jnp.where(
        q_lane == 0, ends[0][0], jnp.where(q_lane == 1, ends[0][1],
        jnp.where(q_lane == 2, ends[1][0], ends[1][1])))
    own_weights = jnp.where(
        q_lane == 0, ends[0][2], jnp.where(q_lane == 1, ends[0][3],
        jnp.where(q_lane == 2, ends[1][2], ends[1][3])))
    message = jnp.where(row8 == 0, own_ids, jnp.where(row8 == 1, own_weights, 0.0))
    message = jnp.where((lane < 64) & (lane // 8 == z), message, 0.0)
    meta1[...] = message
    meta1_in[z] = message

    step(1)
    step(2)
    pl.semaphore_wait(barrier, len(peers))
    gather_start(meta1, meta1_in.at[z], z_peers, 0)
    step(3)
    step(4)
    step(5)

    wait_bytes(meta1_in.at[pl.ds(0, NZ - 1)], recv_sem.at[0])
    line = jnp.sum(meta1_in[...], axis=0)
    line_ids, line_w = line[0:1], line[1:2]
    odd = row8 % 2 == 1
    targ = jnp.sum(
        jnp.where(lane == row8 + jnp.where(odd, 56, 0), line_ids, 0.0), axis=1, keepdims=True
    )
    before = jnp.sum(jnp.where(lane == row8 - 1, line_ids, 0.0), axis=1, keepdims=True)
    group = (lane < 64) & ((lane % 8) // 2 == row8 // 2)
    keep = jnp.logical_not(odd) | (targ != before)
    spread = jnp.where(group & keep & (line_ids == targ), 1.0, 0.0)
    line_weight = jnp.sum(spread * line_w, axis=1, keepdims=True)
    place = lane == 64 + x * 8 + row8
    put_ids = jnp.sum(jnp.where(place, targ, 0.0), axis=0, keepdims=True)
    put_w = jnp.sum(jnp.where(place, line_weight, 0.0), axis=0, keepdims=True)
    message = jnp.where(row8 == 0, put_ids, jnp.where(row8 == 1, put_w, 0.0))
    meta2[...] = message
    meta2_in[x] = message
    coef_d[...] = (spread + pltpu.roll(spread, 64, 1)).astype(BF16)
    gather_start(meta2, meta2_in.at[x], x_peers, 1)
    step(6)


    def weighted(new, index):
        m = mask[index]
        return [
            jnp.sum(new[:, 128 * i : 128 * i + 128] * m, axis=0, keepdims=True)
            for i in range(2)
        ]

    roots = jnp.where(row8 == 4, weight_sum, 0.0)
    for j in range(2):
        for i, part in enumerate(weighted(block(j, 1, 0, True), 4)):
            roots = jnp.where(row8 == 2 * j + i, part, roots)
    root1[...] = roots
    root1_in[z] = roots
    gather_start(root1, root1_in.at[z], z_peers, 4)
    halves = [jnp.zeros((8, 128), F32), jnp.zeros((8, 128), F32)]
    for j in range(2, 6):
        t, h = (j - 2) // 2, (j - 2) % 2
        new = block(j, 1, 0, True)
        for end in range(2):
            for i, part in enumerate(weighted(new, 2 * t + end)):
                halves[i] = jnp.where(row8 == 4 * h + 2 * t + end, part, halves[i])
    nodes = jnp.concatenate(halves, axis=1)
    pay1[...] = nodes
    pay1_in[z] = nodes
    gather_start(pay1, pay1_in.at[z], z_peers, 2)
    for j in range(6, NBLK):
        block(j, 1, 0, True)

    wait_bytes(meta2_in.at[pl.ds(0, NX - 1)], recv_sem.at[1])
    table = line + jnp.sum(meta2_in[...], axis=0)
    all_ids, all_w = table[0:1], table[1:2]
    wide = lax.broadcasted_iota(jnp.int32, (ROWS, 128), 1)
    other = ((wide < 64) & (wide // 8 != z)) | (
        (wide >= 64) & (wide < 96) & ((wide - 64) // 8 != x)
    )
    for t in range(2):
        match = (id_cols[t] == all_ids) & other & ((wide % 4) // 2 == t)
        for h in range(2):
            part = jnp.where(match & ((wide % 8) // 4 == h), 1.0, 0.0)
            if h == 0:
                total = local_totals[t] + jnp.sum(part * all_w, axis=1, keepdims=True)
                inv[:, 128 * t : 128 * t + 128] = jnp.broadcast_to(1.0 / total, (ROWS, 128))
            half = part.astype(BF16)
            q = 2 * t + h
            coef_c[q * ROWS : (q + 1) * ROWS] = jnp.concatenate([half, half], axis=1)

    for t in range(2):
        for h in range(2):
            c = SEC * (t + 1) + BLK * h
            s = slice(c, c + BLK)
            local = mm(coef_l[t], stack3(box[:, s]))
            scale = inv[:, 128 * t : 128 * t + 1]
            nm[:, s] = mult[:, s] + pen[:, s] * (box[:, s] - local * scale)
    nm[:, :SEC] = mult[:, :SEC] + pen[:, :SEC] * box[:, :SEC]

    wait_bytes(root1_in.at[pl.ds(0, NZ - 1)], recv_sem.at[4])
    roots = jnp.sum(root1_in[...], axis=0)
    root2[...] = roots
    root2_in[x * NY + y] = roots
    gather_start(root2, root2_in.at[x * NY + y], xy_peers, 5)

    wait_bytes(pay1_in.at[pl.ds(0, NZ - 1)], recv_sem.at[2])
    hi1, lo1 = split2(pay1_in[...].reshape(NZ * 8, BLK))
    nodes = mm(coef_d[...], jnp.concatenate([hi1, lo1], axis=0))
    pay2[...] = nodes
    pay2_in[x] = nodes
    gather_start(pay2, pay2_in.at[x], x_peers, 3)

    wait_bytes(pay2_in.at[pl.ds(0, NX - 1)], recv_sem.at[3])
    hi2, lo2 = split2(pay2_in[...].reshape(NX * 8, BLK))
    none = jnp.zeros((32, BLK), BF16)
    stacked = jnp.concatenate([hi1, hi2, none, lo1, lo2, none], axis=0)
    remote = mm(coef_c[...], stacked)
    for t in range(2):
        for h in range(2):
            c = SEC * (t + 1) + BLK * h
            s = slice(c, c + BLK)
            q = 2 * t + h
            scale = inv[:, 128 * t : 128 * t + 1]
            nm[:, s] = nm[:, s] - pen[:, s] * (remote[q * ROWS : (q + 1) * ROWS] * scale)

    wait_bytes(root2_in.at[pl.ds(0, NX * NY - 1)], recv_sem.at[5])
    roots = jnp.sum(root2_in[...], axis=0)
    root3[...] = roots
    gather_start(root3, root3_in, c_peers, 6)
    wait_bytes(root3_in, recv_sem.at[6])
    roots = roots + root3_in[...]
    means = roots / roots[4:5]
    for r in range(4):
        s = slice(128 * r, 128 * r + 128)
        nm[:, s] = nm[:, s] - pen[:, s] * means[r : r + 1]

    for index, ref in enumerate((
        meta1_in.at[pl.ds(0, NZ - 1)], meta2_in.at[pl.ds(0, NX - 1)],
        pay1_in.at[pl.ds(0, NZ - 1)], pay2_in.at[pl.ds(0, NX - 1)],
        root1_in.at[pl.ds(0, NZ - 1)], root2_in.at[pl.ds(0, NX * NY - 1)], root3_in,
    )):
        wait_bytes(ref, send_sem.at[index])


def on_device(
    kkt_inverse, cost, anchor, capacity, multiplier, penalty, weight, node_two, node_three
):
    anywhere = pl.BlockSpec(memory_space=pl.ANY)
    vm = pltpu.VMEM
    return pl.pallas_call(
        kernel,
        out_shape=(
            jax.ShapeDtypeStruct((ROWS, NV), F32),
            jax.ShapeDtypeStruct((ROWS, 3 * SEC), F32),
        ),
        in_specs=[anywhere] * 9,
        out_specs=(pl.BlockSpec(memory_space=vm), pl.BlockSpec(memory_space=vm)),
        scratch_shapes=[
            vm((NV, NV), BF16), vm((ROWS, NV), F32), vm((ROWS, NV), F32), vm((ROWS, NV), F32),
            vm((ROWS, 3 * SEC), F32), vm((1, NV), F32),
            vm((1, ROWS), jnp.int32), vm((1, ROWS), jnp.int32), vm((1, ROWS), jnp.int32),
            vm((ROWS, NV), F32), vm((ROWS, NV), F32), vm((2, ROWS, NV), BF16),
            vm((2, ROWS, 192), BF16), vm((4 * ROWS, 256), BF16), vm((8, 128), BF16),
            vm((5, ROWS, 128), F32), vm((ROWS, 256), F32),
            vm((8, 128), F32), vm((NZ, 8, 128), F32), vm((8, 128), F32), vm((NX, 8, 128), F32),
            vm((8, BLK), F32), vm((NZ, 8, BLK), F32), vm((8, BLK), F32), vm((NX, 8, BLK), F32),
            vm((8, 128), F32), vm((NZ, 8, 128), F32),
            vm((8, 128), F32), vm((NX * NY, 8, 128), F32),
            vm((8, 128), F32), vm((8, 128), F32),
            pltpu.SemaphoreType.DMA((8,)), pltpu.SemaphoreType.DMA((NBLK,)),
            pltpu.SemaphoreType.DMA((7,)), pltpu.SemaphoreType.DMA((7,)),
        ],
        compiler_params=pltpu.CompilerParams(
            collective_id=0, has_side_effects=True, vmem_limit_bytes=24 << 20
        ),
        cost_estimate=pl.CostEstimate(
            flops=2 * ITERS * ROWS * NV * NV, bytes_accessed=12 << 20, transcendentals=0
        ),
    )(*(
        pltpu.with_memory_space_constraint(a, pltpu.HBM)
        for a in (
            kkt_inverse, cost, anchor, capacity, multiplier, penalty.reshape(1, NV),
            weight.reshape(1, ROWS), node_two.reshape(1, ROWS), node_three.reshape(1, ROWS),
        )
    ))


def solution(mesh):
    rows = P(("branch", "slot"), None)
    flat = P(("branch", "slot"))
    return jax.shard_map(
        on_device,
        mesh=mesh,
        in_specs=(P(), rows, rows, rows, rows, P(), flat, flat, flat),
        out_specs=(rows, rows),
        check_vma=False,
    )
```

```python
import functools

import jax
import jax.numpy as jnp
from jax import lax
from jax.experimental import pallas as pl
from jax.experimental.pallas import tpu as pltpu
from jax.sharding import PartitionSpec as P

ITERS = 8
ROWS = 64
NV = 2048
SEC = 512
BLK = 256
NBLK = NV // BLK
NX, NY, NZ, NC = 4, 4, 8, 2
F32 = jnp.float32
BF16 = jnp.bfloat16
XY_FAR_FIRST = (
    (2, 2), (2, 1), (2, 3), (1, 2), (3, 2), (2, 0), (0, 2), (1, 1), (1, 3), (3, 1), (3, 3),
    (1, 0), (3, 0), (0, 1), (0, 3),
)


def split2(v):
    hi = v.astype(BF16)
    lo = (v - hi.astype(F32)).astype(BF16)
    return hi, lo


def stack3(v):
    hi, lo = split2(v)
    rest = (v - hi.astype(F32) - lo.astype(F32)).astype(BF16)
    return jnp.concatenate([hi, lo, rest], axis=0)


def mm(a, b):
    return jnp.dot(a, b, preferred_element_type=F32)


def triple(a):
    a = a.astype(BF16)
    return jnp.concatenate([a, a, a], axis=1)


def wait_bytes(ref, sem):
    pltpu.make_async_copy(ref, ref, sem).wait()


def kernel(
    k_h, cost_h, anchor_h, cap_h, mult_h, pen_h, w_h, n2_h, n3_h,
    box, nm,
    kv, cost, anchor, cap, mult, pen, wv, n2v, n3v,
    lin, sc, rhs,
    coef_l, coef_c, coef_d, mask, inv,
    meta1, meta1_in, meta2, meta2_in,
    pay1, pay1_in, pay2, pay2_in,
    root1, root1_in, root2, root2_in, root3, root3_in,
    in_sem, k_sem, send_sem, recv_sem,
):
    slot = lax.axis_index("slot")
    branch = lax.axis_index("branch")
    x, z = slot // NZ, slot % NZ
    y, core = branch // NC, branch % NC

    z_peers = [{"slot": x * NZ + (z + d) % NZ} for d in (4, 3, 5, 2, 6, 1, 7)]
    x_peers = [{"slot": ((x + d) % NX) * NZ + z} for d in (2, 1, 3)]
    xy_peers = [
        {"slot": ((x + d) % NX) * NZ + z, "branch": ((y + e) % NY) * NC + core}
        for d, e in XY_FAR_FIRST
    ]
    c_peers = [{"branch": y * NC + 1 - core}]
    peers = z_peers + xy_peers + c_peers

    ins = [
        pltpu.make_async_copy(a, b, in_sem.at[i])
        for i, (a, b) in enumerate((
            (cost_h, cost), (anchor_h, anchor), (mult_h, mult), (pen_h, pen), (cap_h, cap),
            (w_h, wv), (n2_h, n2v), (n3_h, n3v),
        ))
    ]
    for c in ins:
        c.start()
    ks = [
        pltpu.make_async_copy(
            k_h.at[:, pl.ds(j * BLK, BLK)], kv.at[:, pl.ds(j * BLK, BLK)], k_sem.at[j]
        )
        for j in range(NBLK)
    ]
    for c in ks:
        c.start()

    barrier = pltpu.get_barrier_semaphore()

    def greet(some):
        for peer in some:
            pl.semaphore_signal(
                barrier, inc=1, device_id=peer, device_id_type=pl.DeviceIdType.MESH
            )

    greet(peers[:10])

    def gather_start(src, dst, peers, index):
        for peer in peers:
            pltpu.make_async_remote_copy(
                src_ref=src, dst_ref=dst, send_sem=send_sem.at[index], recv_sem=recv_sem.at[index],
                device_id=peer, device_id_type=pl.DeviceIdType.MESH,
            ).start()

    for c in ins:
        c.wait()

    start = jnp.clip(anchor[...], 0.0, cap[...])
    lin[:, : 3 * SEC] = (
        cost[:, : 3 * SEC] + mult[...] - pen[:, : 3 * SEC] * anchor[:, : 3 * SEC]
    )
    lin[:, 3 * SEC :] = cost[:, 3 * SEC :] - pen[:, 3 * SEC :] * anchor[:, 3 * SEC :]
    sc[...] = jnp.zeros((ROWS, NV), F32)
    rhs[0] = (start - lin[...]).astype(BF16)
    greet(peers[10:])

    def block(j, cur, nxt, last):
        s = slice(j * BLK, (j + 1) * BLK)
        trial = jnp.dot(rhs[cur], kv[:, s], preferred_element_type=F32)
        total = trial + sc[:, s]
        new = jnp.clip(total, 0.0, cap[:, s])
        if last:
            box[:, s] = new
            return new
        rest = total - new
        sc[:, s] = rest
        rhs[nxt, :, s] = ((new - rest) - lin[:, s]).astype(BF16)
        return new

    def step(i):
        for j in range(NBLK):
            if i == 0 and j % 4 == 0:
                for c in ks[j : j + 4]:
                    c.wait()
            block(j, i % 2, 1 - i % 2, False)

    step(0)

    w_row = wv[...].astype(F32)
    ids = (n2v[...].astype(F32), n3v[...].astype(F32))
    eye = lax.broadcasted_iota(jnp.int32, (ROWS, ROWS), 0) == lax.broadcasted_iota(
        jnp.int32, (ROWS, ROWS), 1
    )

    def column(row):
        col = jnp.sum(jnp.where(eye, row, 0.0), axis=1, keepdims=True)
        return jnp.broadcast_to(col, (ROWS, 128))

    lane = lax.broadcasted_iota(jnp.int32, (8, 128), 1)
    row8 = lax.broadcasted_iota(jnp.int32, (8, 128), 0)
    id_cols, local_totals, ends = [], [], []
    for t in range(2):
        id_col = jnp.sum(jnp.where(eye, ids[t], 0.0), axis=1, keepdims=True)
        id_cols.append(id_col)
        same = jnp.where(id_col == ids[t], w_row, 0.0)
        coef_l[t] = triple(same)
        local_totals.append(jnp.sum(same, axis=1, keepdims=True))
        first, final = ids[t][:, 0:1], ids[t][:, ROWS - 1 : ROWS]
        at_first = jnp.where(ids[t] == first, w_row, 0.0)
        at_final = jnp.where((ids[t] == final) & (final != first), w_row, 0.0)
        ends.append((first, final, jnp.sum(at_first, axis=1, keepdims=True),
                     jnp.sum(at_final, axis=1, keepdims=True)))
        mask[2 * t] = column(at_first)
        mask[2 * t + 1] = column(at_final)
    mask[4] = column(w_row)
    weight_sum = jnp.sum(w_row, axis=1, keepdims=True)

    q_lane = lane % 4
    own_ids = jnp.where(
        q_lane == 0, ends[0][0], jnp.where(q_lane == 1, ends[0][1],
        jnp.where(q_lane == 2, ends[1][0], ends[1][1])))
    own_weights = jnp.where(
        q_lane == 0, ends[0][2], jnp.where(q_lane == 1, ends[0][3],
        jnp.where(q_lane == 2, ends[1][2], ends[1][3])))
    message = jnp.where(row8 == 0, own_ids, jnp.where(row8 == 1, own_weights, 0.0))
    message = jnp.where((lane < 64) & (lane // 8 == z), message, 0.0)
    meta1[...] = message
    meta1_in[z] = message

    step(1)
    step(2)
    pl.semaphore_wait(barrier, len(peers))
    gather_start(meta1, meta1_in.at[z], z_peers, 0)
    step(3)
    step(4)
    step(5)

    wait_bytes(meta1_in.at[pl.ds(0, NZ - 1)], recv_sem.at[0])
    line = jnp.sum(meta1_in[...], axis=0)
    line_ids, line_w = line[0:1], line[1:2]
    odd = row8 % 2 == 1
    targ = jnp.sum(
        jnp.where(lane == row8 + jnp.where(odd, 56, 0), line_ids, 0.0), axis=1, keepdims=True
    )
    before = jnp.sum(jnp.where(lane == row8 - 1, line_ids, 0.0), axis=1, keepdims=True)
    group = (lane < 64) & ((lane % 8) // 2 == row8 // 2)
    keep = jnp.logical_not(odd) | (targ != before)
    spread = jnp.where(group & keep & (line_ids == targ), 1.0, 0.0)
    line_weight = jnp.sum(spread * line_w, axis=1, keepdims=True)
    place = lane == 64 + x * 8 + row8
    put_ids = jnp.sum(jnp.where(place, targ, 0.0), axis=0, keepdims=True)
    put_w = jnp.sum(jnp.where(place, line_weight, 0.0), axis=0, keepdims=True)
    message = jnp.where(row8 == 0, put_ids, jnp.where(row8 == 1, put_w, 0.0))
    meta2[...] = message
    meta2_in[x] = message
    coef_d[...] = (spread + pltpu.roll(spread, 64, 1)).astype(BF16)
    gather_start(meta2, meta2_in.at[x], x_peers, 1)
    step(6)


    def weighted(new, index):
        m = mask[index]
        return [
            jnp.sum(new[:, 128 * i : 128 * i + 128] * m, axis=0, keepdims=True)
            for i in range(2)
        ]

    roots = jnp.where(row8 == 4, weight_sum, 0.0)
    for j in range(2):
        for i, part in enumerate(weighted(block(j, 1, 0, True), 4)):
            roots = jnp.where(row8 == 2 * j + i, part, roots)
    root1[...] = roots
    root1_in[z] = roots
    gather_start(root1, root1_in.at[z], z_peers, 4)
    halves = [jnp.zeros((8, 128), F32), jnp.zeros((8, 128), F32)]
    for j in range(2, 6):
        t, h = (j - 2) // 2, (j - 2) % 2
        new = block(j, 1, 0, True)
        for end in range(2):
            for i, part in enumerate(weighted(new, 2 * t + end)):
                halves[i] = jnp.where(row8 == 4 * h + 2 * t + end, part, halves[i])
    nodes = jnp.concatenate(halves, axis=1)
    pay1[...] = nodes
    pay1_in[z] = nodes
    gather_start(pay1, pay1_in.at[z], z_peers, 2)
    for j in range(6, NBLK):
        block(j, 1, 0, True)

    wait_bytes(meta2_in.at[pl.ds(0, NX - 1)], recv_sem.at[1])
    table = line + jnp.sum(meta2_in[...], axis=0)
    all_ids, all_w = table[0:1], table[1:2]
    wide = lax.broadcasted_iota(jnp.int32, (ROWS, 128), 1)
    other = ((wide < 64) & (wide // 8 != z)) | (
        (wide >= 64) & (wide < 96) & ((wide - 64) // 8 != x)
    )
    for t in range(2):
        match = (id_cols[t] == all_ids) & other & ((wide % 4) // 2 == t)
        for h in range(2):
            part = jnp.where(match & ((wide % 8) // 4 == h), 1.0, 0.0)
            if h == 0:
                total = local_totals[t] + jnp.sum(part * all_w, axis=1, keepdims=True)
                inv[:, 128 * t : 128 * t + 128] = jnp.broadcast_to(1.0 / total, (ROWS, 128))
            half = part.astype(BF16)
            q = 2 * t + h
            coef_c[q * ROWS : (q + 1) * ROWS] = jnp.concatenate([half, half], axis=1)

    for t in range(2):
        for h in range(2):
            c = SEC * (t + 1) + BLK * h
            s = slice(c, c + BLK)
            local = mm(coef_l[t], stack3(box[:, s]))
            scale = inv[:, 128 * t : 128 * t + 1]
            nm[:, s] = mult[:, s] + pen[:, s] * (box[:, s] - local * scale)
    nm[:, :SEC] = mult[:, :SEC] + pen[:, :SEC] * box[:, :SEC]

    wait_bytes(root1_in.at[pl.ds(0, NZ - 1)], recv_sem.at[4])
    roots = jnp.sum(root1_in[...], axis=0)
    root2[...] = roots
    root2_in[x * NY + y] = roots
    gather_start(root2, root2_in.at[x * NY + y], xy_peers, 5)

    wait_bytes(pay1_in.at[pl.ds(0, NZ - 1)], recv_sem.at[2])
    hi1, lo1 = split2(pay1_in[...].reshape(NZ * 8, BLK))
    nodes = mm(coef_d[...], jnp.concatenate([hi1, lo1], axis=0))
    pay2[...] = nodes
    pay2_in[x] = nodes
    gather_start(pay2, pay2_in.at[x], x_peers, 3)

    wait_bytes(pay2_in.at[pl.ds(0, NX - 1)], recv_sem.at[3])
    hi2, lo2 = split2(pay2_in[...].reshape(NX * 8, BLK))
    none = jnp.zeros((32, BLK), BF16)
    stacked = jnp.concatenate([hi1, hi2, none, lo1, lo2, none], axis=0)
    remote = mm(coef_c[...], stacked)
    for t in range(2):
        for h in range(2):
            c = SEC * (t + 1) + BLK * h
            s = slice(c, c + BLK)
            q = 2 * t + h
            scale = inv[:, 128 * t : 128 * t + 1]
            nm[:, s] = nm[:, s] - pen[:, s] * (remote[q * ROWS : (q + 1) * ROWS] * scale)

    wait_bytes(root2_in.at[pl.ds(0, NX * NY - 1)], recv_sem.at[5])
    roots = jnp.sum(root2_in[...], axis=0)
    root3[...] = roots
    gather_start(root3, root3_in, c_peers, 6)
    wait_bytes(root3_in, recv_sem.at[6])
    roots = roots + root3_in[...]
    means = roots / roots[4:5]
    for r in range(4):
        s = slice(128 * r, 128 * r + 128)
        nm[:, s] = nm[:, s] - pen[:, s] * means[r : r + 1]

    for index, ref in enumerate((
        meta1_in.at[pl.ds(0, NZ - 1)], meta2_in.at[pl.ds(0, NX - 1)],
        pay1_in.at[pl.ds(0, NZ - 1)], pay2_in.at[pl.ds(0, NX - 1)],
        root1_in.at[pl.ds(0, NZ - 1)], root2_in.at[pl.ds(0, NX * NY - 1)], root3_in,
    )):
        wait_bytes(ref, send_sem.at[index])


def on_device(
    kkt_inverse, cost, anchor, capacity, multiplier, penalty, weight, node_two, node_three
):
    anywhere = pl.BlockSpec(memory_space=pl.ANY)
    vm = pltpu.VMEM
    return pl.pallas_call(
        kernel,
        out_shape=(
            jax.ShapeDtypeStruct((ROWS, NV), F32),
            jax.ShapeDtypeStruct((ROWS, 3 * SEC), F32),
        ),
        in_specs=[anywhere] * 9,
        out_specs=(pl.BlockSpec(memory_space=vm), pl.BlockSpec(memory_space=vm)),
        scratch_shapes=[
            vm((NV, NV), BF16), vm((ROWS, NV), F32), vm((ROWS, NV), F32), vm((ROWS, NV), F32),
            vm((ROWS, 3 * SEC), F32), vm((1, NV), F32),
            vm((1, ROWS), jnp.int32), vm((1, ROWS), jnp.int32), vm((1, ROWS), jnp.int32),
            vm((ROWS, NV), F32), vm((ROWS, NV), F32), vm((2, ROWS, NV), BF16),
            vm((2, ROWS, 192), BF16), vm((4 * ROWS, 256), BF16), vm((8, 128), BF16),
            vm((5, ROWS, 128), F32), vm((ROWS, 256), F32),
            vm((8, 128), F32), vm((NZ, 8, 128), F32), vm((8, 128), F32), vm((NX, 8, 128), F32),
            vm((8, BLK), F32), vm((NZ, 8, BLK), F32), vm((8, BLK), F32), vm((NX, 8, BLK), F32),
            vm((8, 128), F32), vm((NZ, 8, 128), F32),
            vm((8, 128), F32), vm((NX * NY, 8, 128), F32),
            vm((8, 128), F32), vm((8, 128), F32),
            pltpu.SemaphoreType.DMA((8,)), pltpu.SemaphoreType.DMA((NBLK,)),
            pltpu.SemaphoreType.DMA((7,)), pltpu.SemaphoreType.DMA((7,)),
        ],
        compiler_params=pltpu.CompilerParams(
            collective_id=0, has_side_effects=True, vmem_limit_bytes=24 << 20
        ),
        cost_estimate=pl.CostEstimate(
            flops=2 * ITERS * ROWS * NV * NV, bytes_accessed=12 << 20, transcendentals=0
        ),
    )(*(
        pltpu.with_memory_space_constraint(a, pltpu.HBM)
        for a in (
            kkt_inverse, cost, anchor, capacity, multiplier, penalty.reshape(1, NV),
            weight.reshape(1, ROWS), node_two.reshape(1, ROWS), node_three.reshape(1, ROWS),
        )
    ))


def solution(mesh):
    rows = P(("branch", "slot"), None)
    flat = P(("branch", "slot"))
    return jax.shard_map(
        on_device,
        mesh=mesh,
        in_specs=(P(), rows, rows, rows, rows, P(), flat, flat, flat),
        out_specs=(rows, rows),
        check_vma=False,
    )
```

```python
import functools

import jax
import jax.numpy as jnp
from jax import lax
from jax.experimental import pallas as pl
from jax.experimental.pallas import tpu as pltpu
from jax.sharding import PartitionSpec as P

ITERS = 8
ROWS = 64
NV = 2048
SEC = 512
BLK = 256
NBLK = NV // BLK
NX, NY, NZ, NC = 4, 4, 8, 2
F32 = jnp.float32
BF16 = jnp.bfloat16
XY_FAR_FIRST = (
    (2, 2), (2, 1), (2, 3), (1, 2), (3, 2), (2, 0), (0, 2), (1, 1), (1, 3), (3, 1), (3, 3),
    (1, 0), (3, 0), (0, 1), (0, 3),
)


def split2(v):
    hi = v.astype(BF16)
    lo = (v - hi.astype(F32)).astype(BF16)
    return hi, lo


def stack3(v):
    hi, lo = split2(v)
    rest = (v - hi.astype(F32) - lo.astype(F32)).astype(BF16)
    return jnp.concatenate([hi, lo, rest], axis=0)


def mm(a, b):
    return jnp.dot(a, b, preferred_element_type=F32)


def triple(a):
    a = a.astype(BF16)
    return jnp.concatenate([a, a, a], axis=1)


def wait_bytes(ref, sem):
    pltpu.make_async_copy(ref, ref, sem).wait()


def kernel(
    k_h, cost_h, anchor_h, cap_h, mult_h, pen_h, w_h, n2_h, n3_h,
    box, nm,
    kv, cost, anchor, cap, mult, pen, wv, n2v, n3v,
    lin, sc, rhs,
    coef_l, coef_c, coef_d, mask, inv,
    meta1, meta1_in, meta2, meta2_in,
    pay1, pay1_in, pay2, pay2_in,
    root1, root1_in, root2, root2_in, root3, root3_in,
    in_sem, k_sem, send_sem, recv_sem,
):
    slot = lax.axis_index("slot")
    branch = lax.axis_index("branch")
    x, z = slot // NZ, slot % NZ
    y, core = branch // NC, branch % NC

    z_peers = [{"slot": x * NZ + (z + d) % NZ} for d in (4, 3, 5, 2, 6, 1, 7)]
    x_peers = [{"slot": ((x + d) % NX) * NZ + z} for d in (2, 1, 3)]
    xy_peers = [
        {"slot": ((x + d) % NX) * NZ + z, "branch": ((y + e) % NY) * NC + core}
        for d, e in XY_FAR_FIRST
    ]
    c_peers = [{"branch": y * NC + 1 - core}]
    peers = z_peers + xy_peers + c_peers

    ins = [
        pltpu.make_async_copy(a, b, in_sem.at[i])
        for i, (a, b) in enumerate((
            (cost_h, cost), (anchor_h, anchor), (mult_h, mult), (pen_h, pen), (cap_h, cap),
            (w_h, wv), (n2_h, n2v), (n3_h, n3v),
        ))
    ]
    for c in ins:
        c.start()
    ks = [
        pltpu.make_async_copy(
            k_h.at[:, pl.ds(j * BLK, BLK)], kv.at[:, pl.ds(j * BLK, BLK)], k_sem.at[j]
        )
        for j in range(NBLK)
    ]
    for c in ks:
        c.start()

    barrier = pltpu.get_barrier_semaphore()

    def greet(some):
        for peer in some:
            pl.semaphore_signal(
                barrier, inc=1, device_id=peer, device_id_type=pl.DeviceIdType.MESH
            )

    greet(peers[:10])

    def gather_start(src, dst, peers, index):
        for peer in peers:
            pltpu.make_async_remote_copy(
                src_ref=src, dst_ref=dst, send_sem=send_sem.at[index], recv_sem=recv_sem.at[index],
                device_id=peer, device_id_type=pl.DeviceIdType.MESH,
            ).start()

    for c in ins:
        c.wait()

    start = jnp.clip(anchor[...], 0.0, cap[...])
    lin[:, : 3 * SEC] = (
        cost[:, : 3 * SEC] + mult[...] - pen[:, : 3 * SEC] * anchor[:, : 3 * SEC]
    )
    lin[:, 3 * SEC :] = cost[:, 3 * SEC :] - pen[:, 3 * SEC :] * anchor[:, 3 * SEC :]
    sc[...] = jnp.zeros((ROWS, NV), F32)
    rhs[0] = (start - lin[...]).astype(BF16)
    greet(peers[10:])

    def block(j, cur, nxt, last):
        s = slice(j * BLK, (j + 1) * BLK)
        trial = jnp.dot(rhs[cur], kv[:, s], preferred_element_type=F32)
        total = trial + sc[:, s]
        new = jnp.clip(total, 0.0, cap[:, s])
        if last:
            box[:, s] = new
            return new
        rest = total - new
        sc[:, s] = rest
        rhs[nxt, :, s] = ((new - rest) - lin[:, s]).astype(BF16)
        return new

    def step(i):
        for j in range(NBLK):
            if i == 0 and j % 4 == 0:
                for c in ks[j : j + 4]:
                    c.wait()
            block(j, i % 2, 1 - i % 2, False)

    step(0)

    w_row = wv[...].astype(F32)
    ids = (n2v[...].astype(F32), n3v[...].astype(F32))
    eye = lax.broadcasted_iota(jnp.int32, (ROWS, ROWS), 0) == lax.broadcasted_iota(
        jnp.int32, (ROWS, ROWS), 1
    )

    def column(row):
        col = jnp.sum(jnp.where(eye, row, 0.0), axis=1, keepdims=True)
        return jnp.broadcast_to(col, (ROWS, 128))

    lane = lax.broadcasted_iota(jnp.int32, (8, 128), 1)
    row8 = lax.broadcasted_iota(jnp.int32, (8, 128), 0)
    id_cols, local_totals, ends = [], [], []
    for t in range(2):
        id_col = jnp.sum(jnp.where(eye, ids[t], 0.0), axis=1, keepdims=True)
        id_cols.append(id_col)
        same = jnp.where(id_col == ids[t], w_row, 0.0)
        coef_l[t] = triple(same)
        local_totals.append(jnp.sum(same, axis=1, keepdims=True))
        first, final = ids[t][:, 0:1], ids[t][:, ROWS - 1 : ROWS]
        at_first = jnp.where(ids[t] == first, w_row, 0.0)
        at_final = jnp.where((ids[t] == final) & (final != first), w_row, 0.0)
        ends.append((first, final, jnp.sum(at_first, axis=1, keepdims=True),
                     jnp.sum(at_final, axis=1, keepdims=True)))
        mask[2 * t] = column(at_first)
        mask[2 * t + 1] = column(at_final)
    mask[4] = column(w_row)
    weight_sum = jnp.sum(w_row, axis=1, keepdims=True)

    q_lane = lane % 4
    own_ids = jnp.where(
        q_lane == 0, ends[0][0], jnp.where(q_lane == 1, ends[0][1],
        jnp.where(q_lane == 2, ends[1][0], ends[1][1])))
    own_weights = jnp.where(
        q_lane == 0, ends[0][2], jnp.where(q_lane == 1, ends[0][3],
        jnp.where(q_lane == 2, ends[1][2], ends[1][3])))
    message = jnp.where(row8 == 0, own_ids, jnp.where(row8 == 1, own_weights, 0.0))
    message = jnp.where((lane < 64) & (lane // 8 == z), message, 0.0)
    meta1[...] = message
    meta1_in[z] = message

    step(1)
    step(2)
    pl.semaphore_wait(barrier, len(peers))
    gather_start(meta1, meta1_in.at[z], z_peers, 0)
    step(3)
    step(4)
    step(5)

    wait_bytes(meta1_in.at[pl.ds(0, NZ - 1)], recv_sem.at[0])
    line = jnp.sum(meta1_in[...], axis=0)
    line_ids, line_w = line[0:1], line[1:2]
    odd = row8 % 2 == 1
    targ = jnp.sum(
        jnp.where(lane == row8 + jnp.where(odd, 56, 0), line_ids, 0.0), axis=1, keepdims=True
    )
    before = jnp.sum(jnp.where(lane == row8 - 1, line_ids, 0.0), axis=1, keepdims=True)
    group = (lane < 64) & ((lane % 8) // 2 == row8 // 2)
    keep = jnp.logical_not(odd) | (targ != before)
    spread = jnp.where(group & keep & (line_ids == targ), 1.0, 0.0)
    line_weight = jnp.sum(spread * line_w, axis=1, keepdims=True)
    place = lane == 64 + x * 8 + row8
    put_ids = jnp.sum(jnp.where(place, targ, 0.0), axis=0, keepdims=True)
    put_w = jnp.sum(jnp.where(place, line_weight, 0.0), axis=0, keepdims=True)
    message = jnp.where(row8 == 0, put_ids, jnp.where(row8 == 1, put_w, 0.0))
    meta2[...] = message
    meta2_in[x] = message
    coef_d[...] = (spread + pltpu.roll(spread, 64, 1)).astype(BF16)
    gather_start(meta2, meta2_in.at[x], x_peers, 1)
    step(6)


    def weighted(new, index):
        m = mask[index]
        return [
            jnp.sum(new[:, 128 * i : 128 * i + 128] * m, axis=0, keepdims=True)
            for i in range(2)
        ]

    roots = jnp.where(row8 == 4, weight_sum, 0.0)
    for j in range(2):
        for i, part in enumerate(weighted(block(j, 1, 0, True), 4)):
            roots = jnp.where(row8 == 2 * j + i, part, roots)
    root1[...] = roots
    root1_in[z] = roots
    gather_start(root1, root1_in.at[z], z_peers, 4)
    halves = [jnp.zeros((8, 128), F32), jnp.zeros((8, 128), F32)]
    for j in range(2, 6):
        t, h = (j - 2) // 2, (j - 2) % 2
        new = block(j, 1, 0, True)
        for end in range(2):
            for i, part in enumerate(weighted(new, 2 * t + end)):
                halves[i] = jnp.where(row8 == 4 * h + 2 * t + end, part, halves[i])
    nodes = jnp.concatenate(halves, axis=1)
    pay1[...] = nodes
    pay1_in[z] = nodes
    gather_start(pay1, pay1_in.at[z], z_peers, 2)
    for j in range(6, NBLK):
        block(j, 1, 0, True)

    wait_bytes(root1_in.at[pl.ds(0, NZ - 1)], recv_sem.at[4])
    roots = jnp.sum(root1_in[...], axis=0)
    root2[...] = roots
    root2_in[x * NY + y] = roots
    gather_start(root2, root2_in.at[x * NY + y], xy_peers, 5)

    wait_bytes(meta2_in.at[pl.ds(0, NX - 1)], recv_sem.at[1])
    table = line + jnp.sum(meta2_in[...], axis=0)
    all_ids, all_w = table[0:1], table[1:2]
    wide = lax.broadcasted_iota(jnp.int32, (ROWS, 128), 1)
    other = ((wide < 64) & (wide // 8 != z)) | (
        (wide >= 64) & (wide < 96) & ((wide - 64) // 8 != x)
    )
    for t in range(2):
        match = (id_cols[t] == all_ids) & other & ((wide % 4) // 2 == t)
        for h in range(2):
            part = jnp.where(match & ((wide % 8) // 4 == h), 1.0, 0.0)
            if h == 0:
                total = local_totals[t] + jnp.sum(part * all_w, axis=1, keepdims=True)
                inv[:, 128 * t : 128 * t + 128] = jnp.broadcast_to(1.0 / total, (ROWS, 128))
            half = part.astype(BF16)
            q = 2 * t + h
            coef_c[q * ROWS : (q + 1) * ROWS] = jnp.concatenate([half, half], axis=1)

    for t in range(2):
        for h in range(2):
            c = SEC * (t + 1) + BLK * h
            s = slice(c, c + BLK)
            local = mm(coef_l[t], stack3(box[:, s]))
            scale = inv[:, 128 * t : 128 * t + 1]
            nm[:, s] = mult[:, s] + pen[:, s] * (box[:, s] - local * scale)
    nm[:, :SEC] = mult[:, :SEC] + pen[:, :SEC] * box[:, :SEC]

    wait_bytes(pay1_in.at[pl.ds(0, NZ - 1)], recv_sem.at[2])
    hi1, lo1 = split2(pay1_in[...].reshape(NZ * 8, BLK))
    nodes = mm(coef_d[...], jnp.concatenate([hi1, lo1], axis=0))
    pay2[...] = nodes
    pay2_in[x] = nodes
    gather_start(pay2, pay2_in.at[x], x_peers, 3)

    wait_bytes(root2_in.at[pl.ds(0, NX * NY - 1)], recv_sem.at[5])
    roots = jnp.sum(root2_in[...], axis=0)
    root3[...] = roots
    gather_start(root3, root3_in, c_peers, 6)

    wait_bytes(pay2_in.at[pl.ds(0, NX - 1)], recv_sem.at[3])
    hi2, lo2 = split2(pay2_in[...].reshape(NX * 8, BLK))
    none = jnp.zeros((32, BLK), BF16)
    stacked = jnp.concatenate([hi1, hi2, none, lo1, lo2, none], axis=0)
    remote = mm(coef_c[...], stacked)
    for t in range(2):
        for h in range(2):
            c = SEC * (t + 1) + BLK * h
            s = slice(c, c + BLK)
            q = 2 * t + h
            scale = inv[:, 128 * t : 128 * t + 1]
            nm[:, s] = nm[:, s] - pen[:, s] * (remote[q * ROWS : (q + 1) * ROWS] * scale)

    wait_bytes(root3_in, recv_sem.at[6])
    roots = roots + root3_in[...]
    means = roots / roots[4:5]
    for r in range(4):
        s = slice(128 * r, 128 * r + 128)
        nm[:, s] = nm[:, s] - pen[:, s] * means[r : r + 1]

    for index, ref in enumerate((
        meta1_in.at[pl.ds(0, NZ - 1)], meta2_in.at[pl.ds(0, NX - 1)],
        pay1_in.at[pl.ds(0, NZ - 1)], pay2_in.at[pl.ds(0, NX - 1)],
        root1_in.at[pl.ds(0, NZ - 1)], root2_in.at[pl.ds(0, NX * NY - 1)], root3_in,
    )):
        wait_bytes(ref, send_sem.at[index])


def on_device(
    kkt_inverse, cost, anchor, capacity, multiplier, penalty, weight, node_two, node_three
):
    anywhere = pl.BlockSpec(memory_space=pl.ANY)
    vm = pltpu.VMEM
    return pl.pallas_call(
        kernel,
        out_shape=(
            jax.ShapeDtypeStruct((ROWS, NV), F32),
            jax.ShapeDtypeStruct((ROWS, 3 * SEC), F32),
        ),
        in_specs=[anywhere] * 9,
        out_specs=(pl.BlockSpec(memory_space=vm), pl.BlockSpec(memory_space=vm)),
        scratch_shapes=[
            vm((NV, NV), BF16), vm((ROWS, NV), F32), vm((ROWS, NV), F32), vm((ROWS, NV), F32),
            vm((ROWS, 3 * SEC), F32), vm((1, NV), F32),
            vm((1, ROWS), jnp.int32), vm((1, ROWS), jnp.int32), vm((1, ROWS), jnp.int32),
            vm((ROWS, NV), F32), vm((ROWS, NV), F32), vm((2, ROWS, NV), BF16),
            vm((2, ROWS, 192), BF16), vm((4 * ROWS, 256), BF16), vm((8, 128), BF16),
            vm((5, ROWS, 128), F32), vm((ROWS, 256), F32),
            vm((8, 128), F32), vm((NZ, 8, 128), F32), vm((8, 128), F32), vm((NX, 8, 128), F32),
            vm((8, BLK), F32), vm((NZ, 8, BLK), F32), vm((8, BLK), F32), vm((NX, 8, BLK), F32),
            vm((8, 128), F32), vm((NZ, 8, 128), F32),
            vm((8, 128), F32), vm((NX * NY, 8, 128), F32),
            vm((8, 128), F32), vm((8, 128), F32),
            pltpu.SemaphoreType.DMA((8,)), pltpu.SemaphoreType.DMA((NBLK,)),
            pltpu.SemaphoreType.DMA((7,)), pltpu.SemaphoreType.DMA((7,)),
        ],
        compiler_params=pltpu.CompilerParams(
            collective_id=0, has_side_effects=True, vmem_limit_bytes=24 << 20
        ),
        cost_estimate=pl.CostEstimate(
            flops=2 * ITERS * ROWS * NV * NV, bytes_accessed=12 << 20, transcendentals=0
        ),
    )(*(
        pltpu.with_memory_space_constraint(a, pltpu.HBM)
        for a in (
            kkt_inverse, cost, anchor, capacity, multiplier, penalty.reshape(1, NV),
            weight.reshape(1, ROWS), node_two.reshape(1, ROWS), node_three.reshape(1, ROWS),
        )
    ))


def solution(mesh):
    rows = P(("branch", "slot"), None)
    flat = P(("branch", "slot"))
    return jax.shard_map(
        on_device,
        mesh=mesh,
        in_specs=(P(), rows, rows, rows, rows, P(), flat, flat, flat),
        out_specs=(rows, rows),
        check_vma=False,
    )
```

```python
import functools

import jax
import jax.numpy as jnp
from jax import lax
from jax.experimental import pallas as pl
from jax.experimental.pallas import tpu as pltpu
from jax.sharding import PartitionSpec as P

ITERS = 8
ROWS = 64
NV = 2048
SEC = 512
BLK = 256
NBLK = NV // BLK
NX, NY, NZ, NC = 4, 4, 8, 2
F32 = jnp.float32
BF16 = jnp.bfloat16
GROUPS = {0: 4, 4: 7}
XY_FAR_FIRST = (
    (2, 2), (2, 1), (2, 3), (1, 2), (3, 2), (2, 0), (0, 2), (1, 1), (1, 3), (3, 1), (3, 3),
    (1, 0), (3, 0), (0, 1), (0, 3),
)


def split2(v):
    hi = v.astype(BF16)
    lo = (v - hi.astype(F32)).astype(BF16)
    return hi, lo


def stack3(v):
    hi, lo = split2(v)
    rest = (v - hi.astype(F32) - lo.astype(F32)).astype(BF16)
    return jnp.concatenate([hi, lo, rest], axis=0)


def mm(a, b):
    return jnp.dot(a, b, preferred_element_type=F32)


def triple(a):
    a = a.astype(BF16)
    return jnp.concatenate([a, a, a], axis=1)


def wait_bytes(ref, sem):
    pltpu.make_async_copy(ref, ref, sem).wait()


def kernel(
    k_h, cost_h, anchor_h, cap_h, mult_h, pen_h, w_h, n2_h, n3_h,
    box, nm,
    kv, cost, anchor, cap, mult, pen, wv, n2v, n3v,
    lin, sc, rhs,
    coef_l, coef_c, coef_d, mask, inv,
    meta1, meta1_in, meta2, meta2_in,
    pay1, pay1_in, pay2, pay2_in,
    root1, root1_in, root2, root2_in, root3, root3_in,
    in_sem, k_sem, send_sem, recv_sem,
):
    slot = lax.axis_index("slot")
    branch = lax.axis_index("branch")
    x, z = slot // NZ, slot % NZ
    y, core = branch // NC, branch % NC

    z_peers = [{"slot": x * NZ + (z + d) % NZ} for d in (4, 3, 5, 2, 6, 1, 7)]
    x_peers = [{"slot": ((x + d) % NX) * NZ + z} for d in (2, 1, 3)]
    xy_peers = [
        {"slot": ((x + d) % NX) * NZ + z, "branch": ((y + e) % NY) * NC + core}
        for d, e in XY_FAR_FIRST
    ]
    c_peers = [{"branch": y * NC + 1 - core}]
    peers = z_peers + xy_peers + c_peers

    ins = [
        pltpu.make_async_copy(a, b, in_sem.at[i])
        for i, (a, b) in enumerate((
            (cost_h, cost), (anchor_h, anchor), (mult_h, mult), (pen_h, pen), (cap_h, cap),
            (w_h, wv), (n2_h, n2v), (n3_h, n3v),
        ))
    ]
    for c in ins:
        c.start()
    ks = [
        pltpu.make_async_copy(
            k_h.at[:, pl.ds(j * BLK, BLK)], kv.at[:, pl.ds(j * BLK, BLK)], k_sem.at[j]
        )
        for j in range(NBLK)
    ]
    for c in ks:
        c.start()

    barrier = pltpu.get_barrier_semaphore()

    def greet(some):
        for peer in some:
            pl.semaphore_signal(
                barrier, inc=1, device_id=peer, device_id_type=pl.DeviceIdType.MESH
            )

    greet(peers)

    def gather_start(src, dst, peers, index):
        for peer in peers:
            pltpu.make_async_remote_copy(
                src_ref=src, dst_ref=dst, send_sem=send_sem.at[index], recv_sem=recv_sem.at[index],
                device_id=peer, device_id_type=pl.DeviceIdType.MESH,
            ).start()

    for c in ins:
        c.wait()

    start = jnp.clip(anchor[...], 0.0, cap[...])
    lin[:, : 3 * SEC] = (
        cost[:, : 3 * SEC] + mult[...] - pen[:, : 3 * SEC] * anchor[:, : 3 * SEC]
    )
    lin[:, 3 * SEC :] = cost[:, 3 * SEC :] - pen[:, 3 * SEC :] * anchor[:, 3 * SEC :]
    sc[...] = jnp.zeros((ROWS, NV), F32)
    rhs[0] = (start - lin[...]).astype(BF16)

    def block(j, cur, nxt, last):
        s = slice(j * BLK, (j + 1) * BLK)
        trial = jnp.dot(rhs[cur], kv[:, s], preferred_element_type=F32)
        total = trial + sc[:, s]
        new = jnp.clip(total, 0.0, cap[:, s])
        if last:
            box[:, s] = new
            return new
        rest = total - new
        sc[:, s] = rest
        rhs[nxt, :, s] = ((new - rest) - lin[:, s]).astype(BF16)
        return new

    def step(i, first=0, end=NBLK):
        for j in range(first, end):
            if i == 0 and j in GROUPS:
                for c in ks[j : GROUPS[j]]:
                    c.wait()
            block(j, i % 2, 1 - i % 2, False)

    w_row = wv[...].astype(F32)
    ids = (n2v[...].astype(F32), n3v[...].astype(F32))
    eye = lax.broadcasted_iota(jnp.int32, (ROWS, ROWS), 0) == lax.broadcasted_iota(
        jnp.int32, (ROWS, ROWS), 1
    )

    def column(row):
        col = jnp.sum(jnp.where(eye, row, 0.0), axis=1, keepdims=True)
        return jnp.broadcast_to(col, (ROWS, 128))

    lane = lax.broadcasted_iota(jnp.int32, (8, 128), 1)
    row8 = lax.broadcasted_iota(jnp.int32, (8, 128), 0)
    id_cols, local_totals, ends = [], [], []
    for t in range(2):
        id_col = jnp.sum(jnp.where(eye, ids[t], 0.0), axis=1, keepdims=True)
        id_cols.append(id_col)
        same = jnp.where(id_col == ids[t], w_row, 0.0)
        coef_l[t] = triple(same)
        local_totals.append(jnp.sum(same, axis=1, keepdims=True))
        first, final = ids[t][:, 0:1], ids[t][:, ROWS - 1 : ROWS]
        at_first = jnp.where(ids[t] == first, w_row, 0.0)
        at_final = jnp.where((ids[t] == final) & (final != first), w_row, 0.0)
        ends.append((first, final, jnp.sum(at_first, axis=1, keepdims=True),
                     jnp.sum(at_final, axis=1, keepdims=True)))
        mask[2 * t] = column(at_first)
        mask[2 * t + 1] = column(at_final)
    mask[4] = column(w_row)
    weight_sum = jnp.sum(w_row, axis=1, keepdims=True)

    q_lane = lane % 4
    own_ids = jnp.where(
        q_lane == 0, ends[0][0], jnp.where(q_lane == 1, ends[0][1],
        jnp.where(q_lane == 2, ends[1][0], ends[1][1])))
    own_weights = jnp.where(
        q_lane == 0, ends[0][2], jnp.where(q_lane == 1, ends[0][3],
        jnp.where(q_lane == 2, ends[1][2], ends[1][3])))
    message = jnp.where(row8 == 0, own_ids, jnp.where(row8 == 1, own_weights, 0.0))
    message = jnp.where((lane < 64) & (lane // 8 == z), message, 0.0)
    meta1[...] = message
    meta1_in[z] = message

    step(0, 0, NBLK - 1)
    ks[NBLK - 1].wait()
    pl.semaphore_wait(barrier, len(peers))
    gather_start(meta1, meta1_in.at[z], z_peers, 0)
    step(0, NBLK - 1)
    for i in range(1, ITERS - 1):
        step(i)

    def weighted(new, index):
        m = mask[index]
        return [
            jnp.sum(new[:, 128 * i : 128 * i + 128] * m, axis=0, keepdims=True)
            for i in range(2)
        ]

    roots = jnp.where(row8 == 4, weight_sum, 0.0)
    for j in range(2):
        for i, part in enumerate(weighted(block(j, 1, 0, True), 4)):
            roots = jnp.where(row8 == 2 * j + i, part, roots)
    root1[...] = roots
    root1_in[z] = roots
    gather_start(root1, root1_in.at[z], z_peers, 4)
    halves = [jnp.zeros((8, 128), F32), jnp.zeros((8, 128), F32)]
    for j in range(2, 6):
        t, h = (j - 2) // 2, (j - 2) % 2
        new = block(j, 1, 0, True)
        for end in range(2):
            for i, part in enumerate(weighted(new, 2 * t + end)):
                halves[i] = jnp.where(row8 == 4 * h + 2 * t + end, part, halves[i])
    nodes = jnp.concatenate(halves, axis=1)
    pay1[...] = nodes
    pay1_in[z] = nodes
    gather_start(pay1, pay1_in.at[z], z_peers, 2)
    for j in range(6, NBLK):
        block(j, 1, 0, True)

    wait_bytes(meta1_in.at[pl.ds(0, NZ - 1)], recv_sem.at[0])
    line = jnp.sum(meta1_in[...], axis=0)
    line_ids, line_w = line[0:1], line[1:2]
    odd = row8 % 2 == 1
    targ = jnp.sum(
        jnp.where(lane == row8 + jnp.where(odd, 56, 0), line_ids, 0.0), axis=1, keepdims=True
    )
    before = jnp.sum(jnp.where(lane == row8 - 1, line_ids, 0.0), axis=1, keepdims=True)
    group = (lane < 64) & ((lane % 8) // 2 == row8 // 2)
    keep = jnp.logical_not(odd) | (targ != before)
    spread = jnp.where(group & keep & (line_ids == targ), 1.0, 0.0)
    line_weight = jnp.sum(spread * line_w, axis=1, keepdims=True)
    place = lane == 64 + x * 8 + row8
    put_ids = jnp.sum(jnp.where(place, targ, 0.0), axis=0, keepdims=True)
    put_w = jnp.sum(jnp.where(place, line_weight, 0.0), axis=0, keepdims=True)
    message = jnp.where(row8 == 0, put_ids, jnp.where(row8 == 1, put_w, 0.0))
    meta2[...] = message
    meta2_in[x] = message
    coef_d[...] = (spread + pltpu.roll(spread, 64, 1)).astype(BF16)
    gather_start(meta2, meta2_in.at[x], x_peers, 1)


    wait_bytes(root1_in.at[pl.ds(0, NZ - 1)], recv_sem.at[4])
    roots = jnp.sum(root1_in[...], axis=0)
    root2[...] = roots
    root2_in[x * NY + y] = roots
    gather_start(root2, root2_in.at[x * NY + y], xy_peers, 5)

    wait_bytes(meta2_in.at[pl.ds(0, NX - 1)], recv_sem.at[1])
    table = line + jnp.sum(meta2_in[...], axis=0)
    all_ids, all_w = table[0:1], table[1:2]
    wide = lax.broadcasted_iota(jnp.int32, (ROWS, 128), 1)
    other = ((wide < 64) & (wide // 8 != z)) | (
        (wide >= 64) & (wide < 96) & ((wide - 64) // 8 != x)
    )
    for t in range(2):
        match = (id_cols[t] == all_ids) & other & ((wide % 4) // 2 == t)
        for h in range(2):
            part = jnp.where(match & ((wide % 8) // 4 == h), 1.0, 0.0)
            if h == 0:
                total = local_totals[t] + jnp.sum(part * all_w, axis=1, keepdims=True)
                inv[:, 128 * t : 128 * t + 128] = jnp.broadcast_to(1.0 / total, (ROWS, 128))
            half = part.astype(BF16)
            q = 2 * t + h
            coef_c[q * ROWS : (q + 1) * ROWS] = jnp.concatenate([half, half], axis=1)

    for t in range(2):
        for h in range(2):
            c = SEC * (t + 1) + BLK * h
            s = slice(c, c + BLK)
            local = mm(coef_l[t], stack3(box[:, s]))
            scale = inv[:, 128 * t : 128 * t + 1]
            nm[:, s] = mult[:, s] + pen[:, s] * (box[:, s] - local * scale)
    nm[:, :SEC] = mult[:, :SEC] + pen[:, :SEC] * box[:, :SEC]

    wait_bytes(pay1_in.at[pl.ds(0, NZ - 1)], recv_sem.at[2])
    hi1, lo1 = split2(pay1_in[...].reshape(NZ * 8, BLK))
    nodes = mm(coef_d[...], jnp.concatenate([hi1, lo1], axis=0))
    pay2[...] = nodes
    pay2_in[x] = nodes
    gather_start(pay2, pay2_in.at[x], x_peers, 3)

    wait_bytes(root2_in.at[pl.ds(0, NX * NY - 1)], recv_sem.at[5])
    roots = jnp.sum(root2_in[...], axis=0)
    root3[...] = roots
    gather_start(root3, root3_in, c_peers, 6)

    wait_bytes(pay2_in.at[pl.ds(0, NX - 1)], recv_sem.at[3])
    hi2, lo2 = split2(pay2_in[...].reshape(NX * 8, BLK))
    none = jnp.zeros((32, BLK), BF16)
    stacked = jnp.concatenate([hi1, hi2, none, lo1, lo2, none], axis=0)
    remote = mm(coef_c[...], stacked)
    for t in range(2):
        for h in range(2):
            c = SEC * (t + 1) + BLK * h
            s = slice(c, c + BLK)
            q = 2 * t + h
            scale = inv[:, 128 * t : 128 * t + 1]
            nm[:, s] = nm[:, s] - pen[:, s] * (remote[q * ROWS : (q + 1) * ROWS] * scale)

    wait_bytes(root3_in, recv_sem.at[6])
    roots = roots + root3_in[...]
    means = roots / roots[4:5]
    for r in range(4):
        s = slice(128 * r, 128 * r + 128)
        nm[:, s] = nm[:, s] - pen[:, s] * means[r : r + 1]

    for index, ref in enumerate((
        meta1_in.at[pl.ds(0, NZ - 1)], meta2_in.at[pl.ds(0, NX - 1)],
        pay1_in.at[pl.ds(0, NZ - 1)], pay2_in.at[pl.ds(0, NX - 1)],
        root1_in.at[pl.ds(0, NZ - 1)], root2_in.at[pl.ds(0, NX * NY - 1)], root3_in,
    )):
        wait_bytes(ref, send_sem.at[index])


def on_device(
    kkt_inverse, cost, anchor, capacity, multiplier, penalty, weight, node_two, node_three
):
    anywhere = pl.BlockSpec(memory_space=pl.ANY)
    vm = pltpu.VMEM
    return pl.pallas_call(
        kernel,
        out_shape=(
            jax.ShapeDtypeStruct((ROWS, NV), F32),
            jax.ShapeDtypeStruct((ROWS, 3 * SEC), F32),
        ),
        in_specs=[anywhere] * 9,
        out_specs=(pl.BlockSpec(memory_space=vm), pl.BlockSpec(memory_space=vm)),
        scratch_shapes=[
            vm((NV, NV), BF16), vm((ROWS, NV), F32), vm((ROWS, NV), F32), vm((ROWS, NV), F32),
            vm((ROWS, 3 * SEC), F32), vm((1, NV), F32),
            vm((1, ROWS), jnp.int32), vm((1, ROWS), jnp.int32), vm((1, ROWS), jnp.int32),
            vm((ROWS, NV), F32), vm((ROWS, NV), F32), vm((2, ROWS, NV), BF16),
            vm((2, ROWS, 192), BF16), vm((4 * ROWS, 256), BF16), vm((8, 128), BF16),
            vm((5, ROWS, 128), F32), vm((ROWS, 256), F32),
            vm((8, 128), F32), vm((NZ, 8, 128), F32), vm((8, 128), F32), vm((NX, 8, 128), F32),
            vm((8, BLK), F32), vm((NZ, 8, BLK), F32), vm((8, BLK), F32), vm((NX, 8, BLK), F32),
            vm((8, 128), F32), vm((NZ, 8, 128), F32),
            vm((8, 128), F32), vm((NX * NY, 8, 128), F32),
            vm((8, 128), F32), vm((8, 128), F32),
            pltpu.SemaphoreType.DMA((8,)), pltpu.SemaphoreType.DMA((NBLK,)),
            pltpu.SemaphoreType.DMA((7,)), pltpu.SemaphoreType.DMA((7,)),
        ],
        compiler_params=pltpu.CompilerParams(
            collective_id=0, has_side_effects=True, vmem_limit_bytes=24 << 20
        ),
        cost_estimate=pl.CostEstimate(
            flops=2 * ITERS * ROWS * NV * NV, bytes_accessed=12 << 20, transcendentals=0
        ),
    )(*(
        pltpu.with_memory_space_constraint(a, pltpu.HBM)
        for a in (
            kkt_inverse, cost, anchor, capacity, multiplier, penalty.reshape(1, NV),
            weight.reshape(1, ROWS), node_two.reshape(1, ROWS), node_three.reshape(1, ROWS),
        )
    ))


def solution(mesh):
    rows = P(("branch", "slot"), None)
    flat = P(("branch", "slot"))
    return jax.shard_map(
        on_device,
        mesh=mesh,
        in_specs=(P(), rows, rows, rows, rows, P(), flat, flat, flat),
        out_specs=(rows, rows),
        check_vma=False,
    )
```
